32 devices in a mesh: gx: 8 (over y, x, core), gy: 4 (over z).
Axes of the slice: x: 2, y: 2, z: 4, core: 2. Of those that a mesh axis runs over, the one named last changes fastest.
Arguments:
- density: float32 [256, 256, 128], P('gx', 'gy'), may hold values from 0 to 1
- transfer_table: int32 [4, 128], replicated, may hold values from 0 to 255
- shear_x: int32 [2, 256], P(None, 'gx'), may hold values from -16 to 15, as said below
- shear_y: int32 [2, 256], P(None, 'gy'), may hold values from -16 to 15, as said below
- direction: int32 [2, 2], replicated, may hold values from 0 to 1
Outputs:
- image_x: float32 [2, 4, 256, 128], P(None, None, ('gy', 'gx'))
- image_y: float32 [2, 4, 256, 128], P(None, None, ('gx', 'gy'))
The draws below stay inside these ranges and needn't reach their ends.
Inputs may be any that keep to these rules, and one draw needn't show every extreme that they name: `shear_x`: the shift along z of a slice in a view. `shear_y`: the shift along z of a slice in a view.
All inputs are finite; a program needn't handle non-finite values.
Results may differ from the reference program's by a relative error of at most 0.0003.
Values sent between devices are 32-bit elements; how exact they have to be, the bound alone decides.
A program may use at most 192 MiB of HBM per device.

```python
import jax
import jax.numpy as jnp
from jax import lax

NZ = 128
KNOTS = 128
SHEAR = 16
VIEWS = 2
NX = 256
NY = 256


def shear_table(key, length):
    slopes = jax.random.randint(jax.random.fold_in(key, 1), (VIEWS,), -SHEAR, SHEAR + 1)
    starts = jax.random.randint(jax.random.fold_in(key, 2), (VIEWS,), -SHEAR, SHEAR)
    jitter = jax.random.randint(jax.random.fold_in(key, 3), (VIEWS, length), -1, 2)
    positions = jnp.arange(length, dtype=jnp.int32)
    table = starts[:, None] + positions[None, :] * slopes[:, None] // length + jitter
    table = jnp.clip(table, -SHEAR, SHEAR - 1).astype(jnp.int32)
    chosen = jax.random.permutation(jax.random.fold_in(key, 5), VIEWS)
    spots = jax.random.randint(jax.random.fold_in(key, 7), (2,), 0, length)
    table = table.at[chosen[0], spots[0]].set(SHEAR - 1)
    table = table.at[chosen[1], spots[1]].set(-SHEAR)
    return table.astype(jnp.int32)


def draw_shear_x(key, part):
    return shear_table(jax.random.fold_in(key, 17), NX)


def draw_shear_y(key, part):
    return shear_table(jax.random.fold_in(key, 29), NY)


def plant(array, key, smallest, high):
    longest = array.shape.index(max(array.shape))
    spots = []
    for shift in (0, 1):
        where = [jax.random.randint(jax.random.fold_in(key, axis), (), 0, length) for axis, length in enumerate(array.shape)]
        where[longest] = (where[longest] + shift) % array.shape[longest]
        spots.append(tuple(where))
    return array.at[spots[0]].set(smallest).at[spots[1]].set(high)


def block_scale(key, dims, pieces, least, top_value):
    def one(axis_at, shards_of):
        heights = jax.random.uniform(jax.random.fold_in(jax.random.fold_in(key, 6), axis_at), (shards_of,), jnp.float32, least / len(pieces), top_value / len(pieces))
        return jnp.repeat(jnp.exp(heights), dims[axis_at] // shards_of).reshape((-1,) + (1,) * (len(dims) - axis_at - 1))

    gain = one(*pieces[0])
    for cut in pieces[1:]:
        gain = gain * one(*cut)
    return gain


def setup_inputs(seed: int = 0) -> dict:
    arg_keys = jax.random.split(jax.random.key(seed), 6)
    density = jnp.clip(1.0 * jax.random.uniform(arg_keys[0], (NX, NY, NZ), jnp.float32) ** block_scale(arg_keys[0], (NX, NY, NZ), ((0, 8), (1, 4)), -0.2, 0.2), 0.0, 1.0)
    transfer_table = plant(jax.random.randint(arg_keys[1], (4, KNOTS), 0, 256), jax.random.fold_in(arg_keys[1], 1), 0, 255).astype(jnp.int32)
    shear_x = draw_shear_x(jax.random.fold_in(arg_keys[5], 71), 0)
    shear_y = draw_shear_y(jax.random.fold_in(arg_keys[5], 71), 0)
    direction = plant(jax.random.randint(arg_keys[4], (2, VIEWS), 0, 2), jax.random.fold_in(arg_keys[4], 1), 0, 1).astype(jnp.int32)
    return dict(density=density, transfer_table=transfer_table, shear_x=shear_x, shear_y=shear_y, direction=direction)


light_x = 1.0 / 3.0
light_y = 2.0 / 3.0
light_z = 2.0 / 3.0
highest = lax.Precision.HIGHEST

def shading(padded):
    framed = jnp.pad(padded, ((0, 0), (0, 0), (1, 1)))
    grad_x = (framed[2:, 1:-1, 1:-1] - framed[:-2, 1:-1, 1:-1]) * 0.5
    grad_y = (framed[1:-1, 2:, 1:-1] - framed[1:-1, :-2, 1:-1]) * 0.5
    grad_z = (framed[1:-1, 1:-1, 2:] - framed[1:-1, 1:-1, :-2]) * 0.5
    facing = jnp.abs(light_x * grad_x + light_y * grad_y + light_z * grad_z)
    return 0.3 + 0.7 * facing / jnp.sqrt(grad_x * grad_x + grad_y * grad_y + grad_z * grad_z + 0.01)

def lookup(values, transfer_table):
    knot_count = transfer_table.shape[1]
    levels = transfer_table.astype(jnp.float32) / 255.0
    places = jnp.arange(knot_count, dtype=jnp.float32)
    scaled = values * (knot_count - 1.0)
    weights = jnp.maximum(0.0, 1.0 - jnp.abs(places[:, None] - scaled[None, :]))
    return jnp.dot(levels, weights, precision=highest, preferred_element_type=jnp.float32)

def classify(density, transfer_table):

    def one_slice(plane_cells):
        return lookup(plane_cells.reshape(-1), transfer_table).reshape((4,) + plane_cells.shape)
    return lax.map(one_slice, density)

def emission(classed, shaded, step_len):
    optical = step_len * 2.0 * classed[:, 3]
    opacity = 1.0 - jnp.exp(-optical)
    colour = classed[:, :3] * (shaded * opacity)[:, None]
    return jnp.concatenate([colour, optical[:, None]], axis=1)

def shift_slice(slab, offset):
    framed = jnp.pad(slab, ((0, 0), (0, 0), (SHEAR, SHEAR)))
    return lax.dynamic_slice_in_dim(framed, (SHEAR - offset).astype(jnp.int32), slab.shape[2], 2)

def render(fields, offsets, turn_flags):

    def one_view(inputs):
        offset_row, turn_flag = inputs
        sheared = jax.vmap(shift_slice)(fields, offset_row)
        depths = sheared[:, 3]
        running = jnp.cumsum(depths, axis=0)
        summed = running[-1]
        before = jnp.where(turn_flag == 0, running - depths, summed[None] - running)
        colour = lax.optimization_barrier(jnp.sum(jnp.exp(-before)[:, None] * sheared[:, :3], axis=0))
        return jnp.concatenate([colour, (1.0 - jnp.exp(-summed))[None]], axis=0)
    return lax.map(one_view, (offsets, turn_flags))

def reference(density, transfer_table, shear_x, shear_y, direction):
    padded = jnp.pad(density, ((1, 1), (1, 1), (0, 0)))
    shaded = shading(padded)
    classed = classify(density, transfer_table)
    along_x = emission(classed, shaded, 1.0 / NX)
    image_x = render(along_x, shear_x, direction[0])
    along_y = emission(classed, shaded, 1.0 / NY).transpose(2, 1, 0, 3)
    image_y = render(along_y, shear_y, direction[1])
    return (image_x, image_y)
```

```python
import functools
import math

import jax
import jax.numpy as jnp
from jax import lax
from jax.experimental import pallas as pl
from jax.experimental.pallas import tpu as pltpu
from jax.sharding import PartitionSpec as P

MESH = pl.DeviceIdType.MESH
LOG2E = math.log2(math.e)
UNROLL = 4


def take(row, places):
    return jnp.take_along_axis(
        jnp.broadcast_to(row, places.shape), places, axis=1, mode="promise_in_bounds"
    )


def exchange_copy(parts, received, send_sem, recv_sem, axis, me, count, step):
    target = lax.rem(me + step, count)
    return pltpu.make_async_remote_copy(
        src_ref=parts.at[target],
        dst_ref=received.at[me],
        send_sem=send_sem.at[step],
        recv_sem=recv_sem.at[step],
        device_id={axis: target},
        device_id_type=MESH,
    )


def march(fields, shear_ref, direction_ref, family, view, depth, pitch, begin, rows, cells_z):
    lanes = lax.broadcasted_iota(jnp.int32, (rows, cells_z), 1)
    turned = direction_ref[family, view]

    def step(i, carried):
        behind, colours = carried
        place = jnp.where(turned == 0, i, depth - 1 - i)
        shift = shear_ref[view, place]
        amount = jnp.where(shift < 0, shift + cells_z, shift)
        inside = (lanes >= shift) & (lanes < cells_z + shift)
        at = pl.ds(pl.multiple_of(place * pitch + begin, 8), rows)
        sheared = [pltpu.roll(fields[c, at, :], amount, 1) for c in range(4)]
        through = jnp.where(inside, jnp.exp2(-behind), 0.0)
        colours = tuple(total + through * sheared[c] for c, total in enumerate(colours))
        return behind + jnp.where(inside, sheared[3], 0.0), colours

    zero = jnp.zeros((rows, cells_z), jnp.float32)
    return lax.fori_loop(0, depth, step, (zero, (zero, zero, zero)), unroll=UNROLL)


def compose(received, direction_ref, family, count, views, out_ref):
    for view in range(views):
        turned = direction_ref[family, view].astype(jnp.float32)
        depths = [received[i, view * 4 + 3] for i in range(count)]
        lower, upper = [jnp.zeros_like(depths[0])], [jnp.zeros_like(depths[0])]
        for i in range(count):
            lower.append(lower[-1] + depths[i])
            upper.append(upper[-1] + depths[count - 1 - i])
        through = [
            jnp.exp2(-(lower[i] * (1.0 - turned) + upper[count - 1 - i] * turned))
            for i in range(count)
        ]
        for c in range(3):
            total = through[0] * received[0, view * 4 + c]
            for i in range(1, count):
                total += through[i] * received[i, view * 4 + c]
            out_ref[view, c] = total
        out_ref[view, 3] = 1.0 - jnp.exp2(-lower[-1])


def halo_kernel(
    dims, counts, density,
    halo_x_low, halo_x_high, halo_y_low, halo_y_high, face_low, face_high, halo_send, halo_recv,
):
    depth_x, depth_y, cells_z = dims
    count_x, count_y = counts
    me_x, me_y = lax.axis_index("gx"), lax.axis_index("gy")

    last = (depth_x - 1) * depth_y
    halos = []
    barrier = pltpu.get_barrier_semaphore()
    for k, (axis, me, count, delta, src, dst) in enumerate((
        ("gx", me_x, count_x, 1, density.at[pl.ds(last, depth_y), :], halo_x_low),
        ("gx", me_x, count_x, -1, density.at[pl.ds(0, depth_y), :], halo_x_high),
        ("gy", me_y, count_y, 1, face_high, halo_y_low),
        ("gy", me_y, count_y, -1, face_low, halo_y_high),
    )):
        partner = {axis: lax.rem(me + delta + count, count)}
        copy = pltpu.make_async_remote_copy(
            src_ref=src, dst_ref=dst, send_sem=halo_send.at[k], recv_sem=halo_recv.at[k],
            device_id=partner, device_id_type=MESH,
        )
        sends = me < count - 1 if delta == 1 else me > 0
        receives = me > 0 if delta == 1 else me < count - 1
        halos.append((copy, sends, receives, dst))

        @pl.when(sends)
        def _():
            pl.semaphore_signal(barrier, inc=1, device_id=partner, device_id_type=MESH)

    face_low[...] = density[pl.ds(0, depth_x, stride=depth_y), :]
    face_high[...] = density[pl.ds(depth_y - 1, depth_x, stride=depth_y), :]
    pl.semaphore_wait(barrier, sum(sends.astype(jnp.int32) for _, sends, _, _ in halos))

    for copy, sends, receives, dst in halos:
        pl.when(sends)(copy.start)

        @pl.when(jnp.logical_not(receives))
        def _():
            dst[...] = jnp.zeros_like(dst)

    for copy, sends, receives, dst in halos:
        pl.when(receives)(copy.wait_recv)
        pl.when(sends)(copy.wait_send)


def brick_kernel(
    dims, counts,
    density, table, shear_x, shear_y, direction,
    halo_x_low, halo_x_high, halo_y_low, halo_y_high,
    parts_x, parts_y, fields_x, fields_y,
):
    depth_x, depth_y, cells_z = dims
    count_x, count_y = counts
    views = shear_x.shape[0]
    knots = table.shape[1]

    step_x = 2.0 * LOG2E / (depth_x * count_x)
    step_y = 2.0 * LOG2E / (depth_y * count_y)
    levels = table[...].astype(jnp.float32) * (1.0 / 255.0)
    rises = pltpu.roll(levels, knots - 1, 1) - levels

    def classify(x, _):
        at = pl.ds(pl.multiple_of(x * depth_y, 8), depth_y)
        scaled = density[at, :] * (knots - 1.0)
        places = jnp.minimum(scaled.astype(jnp.int32), knots - 1)
        rest = scaled - places.astype(jnp.float32)
        for c in range(4):
            value = take(levels[c:c + 1], places) + rest * take(rises[c:c + 1], places)
            if c < 3:
                fields_x[c, at, :] = value
            else:
                fields_x[c, at, :] = value * step_x
                fields_y[c, pl.ds(x, depth_y, stride=depth_x), :] = value * step_y
        return 0

    lax.fori_loop(0, depth_x, classify, 0)

    lanes = lax.broadcasted_iota(jnp.int32, (depth_y, cells_z), 1)
    ranks = lax.broadcasted_iota(jnp.int32, (depth_y, cells_z), 0)

    def shade(x, before, here, after):
        low = halo_y_low[pl.ds(x, 1), :]
        high = halo_y_high[pl.ds(x, 1), :]
        rise_x = after - before
        rise_y = jnp.where(ranks == depth_y - 1, high, pltpu.roll(here, depth_y - 1, 0)) - jnp.where(
            ranks == 0, low, pltpu.roll(here, 1, 0)
        )
        rise_z = jnp.where(lanes == cells_z - 1, 0.0, pltpu.roll(here, cells_z - 1, 1)) - jnp.where(
            lanes == 0, 0.0, pltpu.roll(here, 1, 1)
        )
        facing = jnp.abs(rise_x + 2.0 * (rise_y + rise_z)) * (0.7 / 3.0)
        steep = rise_x * rise_x + rise_y * rise_y + rise_z * rise_z + 0.04
        shaded = 0.3 + facing * lax.rsqrt(steep)
        at = pl.ds(pl.multiple_of(x * depth_y, 8), depth_y)
        turned_at = pl.ds(x, depth_y, stride=depth_x)
        optical = fields_x[3, at, :]
        gain_x = shaded * (1.0 - jnp.exp2(-optical))
        if step_x == step_y:
            gain_y = gain_x
        else:
            gain_y = shaded * (1.0 - jnp.exp2(-(optical * (step_y / step_x))))
        for c in range(3):
            colour = fields_x[c, at, :]
            fields_x[c, at, :] = colour * gain_x
            fields_y[c, turned_at, :] = colour * gain_y

    def plane(x):
        return density[pl.ds(pl.multiple_of(x * depth_y, 8), depth_y), :]

    def shade_inner(x, _):
        shade(x, plane(x - 1), plane(x), plane(x + 1))
        return 0

    shade(0, halo_x_low[...], plane(0), plane(1))
    lax.fori_loop(1, depth_x - 1, shade_inner, 0)
    shade(depth_x - 1, plane(depth_x - 2), plane(depth_x - 1), halo_x_high[...])

    for fields, shear, family, count, depth, across, parts in (
        (fields_x, shear_x, 0, count_x, depth_x, depth_y, parts_x),
        (fields_y, shear_y, 1, count_y, depth_y, depth_x, parts_y),
    ):
        piece = across // count
        rows = math.gcd(across, 32)
        for view in range(views):
            for begin in range(0, across, rows):
                behind, colours = march(
                    fields, shear, direction, family, view, depth, across, begin, rows, cells_z
                )
                for c, result in enumerate(colours + (behind,)):
                    for r in range(0, rows, piece):
                        parts[(begin + r) // piece, view * 4 + c] = result[r:r + piece]


def compose_kernel(
    counts, views, direction, parts_x, parts_y,
    image_x, image_y, got_x, got_y, send_x, recv_x, send_y, recv_y,
):
    count_x, count_y = counts
    me_x, me_y = lax.axis_index("gx"), lax.axis_index("gy")
    barrier = pltpu.get_barrier_semaphore()
    for axis, me, count in (("gx", me_x, count_x), ("gy", me_y, count_y)):
        for step in range(1, count):
            pl.semaphore_signal(
                barrier, inc=1, device_id={axis: lax.rem(me + step, count)}, device_id_type=MESH
            )
    got_x[me_x] = parts_x[me_x]
    got_y[me_y] = parts_y[me_y]
    pl.semaphore_wait(barrier, count_x + count_y - 2)
    groups = []
    for axis, me, count, parts, got, send, recv in (
        ("gx", me_x, count_x, parts_x, got_x, send_x, recv_x),
        ("gy", me_y, count_y, parts_y, got_y, send_y, recv_y),
    ):
        groups.append([
            exchange_copy(parts, got, send, recv, axis, me, count, step) for step in range(1, count)
        ])
        for copy in groups[-1]:
            copy.start()
    for group, family, count, got, image in (
        (groups[1], 1, count_y, got_y, image_y),
        (groups[0], 0, count_x, got_x, image_x),
    ):
        for copy in group:
            copy.wait_recv()
        compose(got, direction, family, count, views, image)
    for group in groups:
        for copy in group:
            copy.wait_send()


def local(density, transfer_table, shear_x, shear_y, direction):
    count_x, count_y = lax.axis_size("gx"), lax.axis_size("gy")
    counts = (count_x, count_y)
    dims = density.shape
    depth_x, depth_y, cells_z = dims
    views = shear_x.shape[0]
    f32 = jnp.float32
    piece_x, piece_y = depth_y // count_x, depth_x // count_y
    cells = depth_x * depth_y
    vmem = pl.BlockSpec(memory_space=pltpu.VMEM)
    smem = pl.BlockSpec(memory_space=pltpu.SMEM)
    density = density.reshape(cells, cells_z)
    layer_x = jax.ShapeDtypeStruct((depth_y, cells_z), f32)
    layer_y = jax.ShapeDtypeStruct((depth_x, cells_z), f32)
    halos = pl.pallas_call(
        functools.partial(halo_kernel, dims, counts),
        out_shape=(layer_x, layer_x, layer_y, layer_y),
        in_specs=[vmem],
        out_specs=(vmem,) * 4,
        scratch_shapes=[
            pltpu.VMEM((depth_x, cells_z), f32),
            pltpu.VMEM((depth_x, cells_z), f32),
            pltpu.SemaphoreType.DMA((4,)),
            pltpu.SemaphoreType.DMA((4,)),
        ],
        compiler_params=pltpu.CompilerParams(collective_id=0, has_side_effects=True),
    )(density)
    parts = pl.pallas_call(
        functools.partial(brick_kernel, dims, counts),
        out_shape=(
            jax.ShapeDtypeStruct((count_x, views * 4, piece_x, cells_z), f32),
            jax.ShapeDtypeStruct((count_y, views * 4, piece_y, cells_z), f32),
        ),
        in_specs=[vmem, vmem, smem, smem, smem] + [vmem] * 4,
        out_specs=(vmem, vmem),
        scratch_shapes=[
            pltpu.VMEM((4, cells, cells_z), f32),
            pltpu.VMEM((4, cells, cells_z), f32),
        ],
        compiler_params=pltpu.CompilerParams(vmem_limit_bytes=40 * 2**20),
    )(density, transfer_table, shear_x, shear_y, direction, *halos)
    return tuple(pl.pallas_call(
        functools.partial(compose_kernel, counts, views),
        out_shape=(
            jax.ShapeDtypeStruct((views, 4, piece_x, cells_z), f32),
            jax.ShapeDtypeStruct((views, 4, piece_y, cells_z), f32),
        ),
        in_specs=[smem, vmem, vmem],
        out_specs=(vmem, vmem),
        scratch_shapes=[
            pltpu.VMEM((count_x, views * 4, piece_x, cells_z), f32),
            pltpu.VMEM((count_y, views * 4, piece_y, cells_z), f32),
            pltpu.SemaphoreType.DMA((count_x,)),
            pltpu.SemaphoreType.DMA((count_x,)),
            pltpu.SemaphoreType.DMA((count_y,)),
            pltpu.SemaphoreType.DMA((count_y,)),
        ],
        compiler_params=pltpu.CompilerParams(collective_id=1, has_side_effects=True),
    )(direction, *parts))


def solution(mesh):
    placed = (P("gx", "gy", None), P(), P(None, "gx"), P(None, "gy"), P())
    return jax.shard_map(
        local,
        mesh=mesh,
        in_specs=placed,
        out_specs=(P(None, None, ("gy", "gx"), None), P(None, None, ("gx", "gy"), None)),
        check_vma=False,
    )
```

```python
import functools
import math

import jax
import jax.numpy as jnp
from jax import lax
from jax.experimental import pallas as pl
from jax.experimental.pallas import tpu as pltpu
from jax.sharding import PartitionSpec as P

MESH = pl.DeviceIdType.MESH
LOG2E = math.log2(math.e)
UNROLL = 16


def take(row, places):
    return jnp.take_along_axis(
        jnp.broadcast_to(row, places.shape), places, axis=1, mode="promise_in_bounds"
    )


def exchange_copy(parts, received, send_sem, recv_sem, axis, me, count, step):
    target = lax.rem(me + step, count)
    return pltpu.make_async_remote_copy(
        src_ref=parts.at[target],
        dst_ref=received.at[me],
        send_sem=send_sem.at[step],
        recv_sem=recv_sem.at[step],
        device_id={axis: target},
        device_id_type=MESH,
    )


def march(fields, shear_ref, direction_ref, family, view, depth, pitch, begin, rows, cells_z):
    lanes = lax.broadcasted_iota(jnp.int32, (rows, cells_z), 1)
    turned = direction_ref[family, view]

    def step(i, carried):
        behind, colours = carried
        place = jnp.where(turned == 0, i, depth - 1 - i)
        shift = shear_ref[view, place]
        amount = jnp.where(shift < 0, shift + cells_z, shift)
        inside = (lanes >= shift) & (lanes < cells_z + shift)
        at = pl.ds(pl.multiple_of(place * pitch + begin, 8), rows)
        sheared = [pltpu.roll(fields[c, at, :], amount, 1) for c in range(4)]
        through = jnp.where(inside, jnp.exp2(-behind), 0.0)
        colours = tuple(total + through * sheared[c] for c, total in enumerate(colours))
        return behind + jnp.where(inside, sheared[3], 0.0), colours

    zero = jnp.zeros((rows, cells_z), jnp.float32)
    return lax.fori_loop(0, depth, step, (zero, (zero, zero, zero)), unroll=UNROLL)


def compose(received, direction_ref, family, count, views, out_ref):
    for view in range(views):
        turned = direction_ref[family, view].astype(jnp.float32)
        depths = [received[i, view * 4 + 3] for i in range(count)]
        lower, upper = [jnp.zeros_like(depths[0])], [jnp.zeros_like(depths[0])]
        for i in range(count):
            lower.append(lower[-1] + depths[i])
            upper.append(upper[-1] + depths[count - 1 - i])
        through = [
            jnp.exp2(-(lower[i] * (1.0 - turned) + upper[count - 1 - i] * turned))
            for i in range(count)
        ]
        for c in range(3):
            total = through[0] * received[0, view * 4 + c]
            for i in range(1, count):
                total += through[i] * received[i, view * 4 + c]
            out_ref[view, c] = total
        out_ref[view, 3] = 1.0 - jnp.exp2(-lower[-1])


def halo_kernel(
    dims, counts, density,
    halo_x_low, halo_x_high, halo_y_low, halo_y_high, face_low, face_high, halo_send, halo_recv,
):
    depth_x, depth_y, cells_z = dims
    count_x, count_y = counts
    me_x, me_y = lax.axis_index("gx"), lax.axis_index("gy")

    last = (depth_x - 1) * depth_y
    halos = []
    barrier = pltpu.get_barrier_semaphore()
    for k, (axis, me, count, delta, src, dst) in enumerate((
        ("gx", me_x, count_x, 1, density.at[pl.ds(last, depth_y), :], halo_x_low),
        ("gx", me_x, count_x, -1, density.at[pl.ds(0, depth_y), :], halo_x_high),
        ("gy", me_y, count_y, 1, face_high, halo_y_low),
        ("gy", me_y, count_y, -1, face_low, halo_y_high),
    )):
        partner = {axis: lax.rem(me + delta + count, count)}
        copy = pltpu.make_async_remote_copy(
            src_ref=src, dst_ref=dst, send_sem=halo_send.at[k], recv_sem=halo_recv.at[k],
            device_id=partner, device_id_type=MESH,
        )
        sends = me < count - 1 if delta == 1 else me > 0
        receives = me > 0 if delta == 1 else me < count - 1
        halos.append((copy, sends, receives, dst))

        @pl.when(sends)
        def _():
            pl.semaphore_signal(barrier, inc=1, device_id=partner, device_id_type=MESH)

    face_low[...] = density[pl.ds(0, depth_x, stride=depth_y), :]
    face_high[...] = density[pl.ds(depth_y - 1, depth_x, stride=depth_y), :]
    pl.semaphore_wait(barrier, sum(sends.astype(jnp.int32) for _, sends, _, _ in halos))

    for copy, sends, receives, dst in halos:
        pl.when(sends)(copy.start)

        @pl.when(jnp.logical_not(receives))
        def _():
            dst[...] = jnp.zeros_like(dst)

    for copy, sends, receives, dst in halos:
        pl.when(receives)(copy.wait_recv)
        pl.when(sends)(copy.wait_send)


def brick_kernel(
    dims, counts,
    density_far, table, shear_x, shear_y, direction,
    far_x_low, far_x_high, far_y_low, far_y_high,
    parts_x, parts_y, fields_x, fields_y, density,
    halo_x_low, halo_x_high, halo_y_low, halo_y_high, loads,
):
    depth_x, depth_y, cells_z = dims
    count_x, count_y = counts
    views = shear_x.shape[0]
    knots = table.shape[1]

    fetches = [
        pltpu.make_async_copy(far, near, loads.at[k])
        for k, (far, near) in enumerate((
            (density_far, density),
            (far_x_low, halo_x_low), (far_x_high, halo_x_high),
            (far_y_low, halo_y_low), (far_y_high, halo_y_high),
        ))
    ]
    for fetch in fetches:
        fetch.start()
    fetches[0].wait()

    step_x = 2.0 * LOG2E / (depth_x * count_x)
    step_y = 2.0 * LOG2E / (depth_y * count_y)
    levels = table[...].astype(jnp.float32) * (1.0 / 255.0)
    rises = pltpu.roll(levels, knots - 1, 1) - levels

    def classify(x, _):
        at = pl.ds(pl.multiple_of(x * depth_y, 8), depth_y)
        scaled = density[at, :] * (knots - 1.0)
        places = jnp.minimum(scaled.astype(jnp.int32), knots - 1)
        rest = scaled - places.astype(jnp.float32)
        for c in range(4):
            value = take(levels[c:c + 1], places) + rest * take(rises[c:c + 1], places)
            if c < 3:
                fields_x[c, at, :] = value
            else:
                fields_x[c, at, :] = value * step_x
                fields_y[c, pl.ds(x, depth_y, stride=depth_x), :] = value * step_y
        return 0

    lax.fori_loop(0, depth_x, classify, 0, unroll=2)

    for fetch in fetches[1:]:
        fetch.wait()
    lanes = lax.broadcasted_iota(jnp.int32, (depth_y, cells_z), 1)
    ranks = lax.broadcasted_iota(jnp.int32, (depth_y, cells_z), 0)

    def shade(x, before, here, after):
        low = halo_y_low[pl.ds(x, 1), :]
        high = halo_y_high[pl.ds(x, 1), :]
        rise_x = after - before
        rise_y = jnp.where(ranks == depth_y - 1, high, pltpu.roll(here, depth_y - 1, 0)) - jnp.where(
            ranks == 0, low, pltpu.roll(here, 1, 0)
        )
        rise_z = jnp.where(lanes == cells_z - 1, 0.0, pltpu.roll(here, cells_z - 1, 1)) - jnp.where(
            lanes == 0, 0.0, pltpu.roll(here, 1, 1)
        )
        facing = jnp.abs(rise_x + 2.0 * (rise_y + rise_z)) * (0.7 / 3.0)
        steep = rise_x * rise_x + rise_y * rise_y + rise_z * rise_z + 0.04
        shaded = 0.3 + facing * lax.rsqrt(steep)
        at = pl.ds(pl.multiple_of(x * depth_y, 8), depth_y)
        turned_at = pl.ds(x, depth_y, stride=depth_x)
        optical = fields_x[3, at, :]
        gain_x = shaded * (1.0 - jnp.exp2(-optical))
        if step_x == step_y:
            gain_y = gain_x
        else:
            gain_y = shaded * (1.0 - jnp.exp2(-(optical * (step_y / step_x))))
        for c in range(3):
            colour = fields_x[c, at, :]
            fields_x[c, at, :] = colour * gain_x
            fields_y[c, turned_at, :] = colour * gain_y

    def plane(x):
        return density[pl.ds(pl.multiple_of(x * depth_y, 8), depth_y), :]

    def shade_inner(x, _):
        shade(x, plane(x - 1), plane(x), plane(x + 1))
        return 0

    shade(0, halo_x_low[...], plane(0), plane(1))
    lax.fori_loop(1, depth_x - 1, shade_inner, 0, unroll=2)
    shade(depth_x - 1, plane(depth_x - 2), plane(depth_x - 1), halo_x_high[...])

    for fields, shear, family, count, depth, across, parts in (
        (fields_x, shear_x, 0, count_x, depth_x, depth_y, parts_x),
        (fields_y, shear_y, 1, count_y, depth_y, depth_x, parts_y),
    ):
        piece = across // count
        rows = math.gcd(across, 32)
        for view in range(views):
            for begin in range(0, across, rows):
                behind, colours = march(
                    fields, shear, direction, family, view, depth, across, begin, rows, cells_z
                )
                for c, result in enumerate(colours + (behind,)):
                    for r in range(0, rows, piece):
                        parts[(begin + r) // piece, view * 4 + c] = result[r:r + piece]


def compose_kernel(
    counts, views, direction, parts_x, parts_y,
    image_x, image_y, got_x, got_y, send_x, recv_x, send_y, recv_y,
):
    count_x, count_y = counts
    me_x, me_y = lax.axis_index("gx"), lax.axis_index("gy")
    barrier = pltpu.get_barrier_semaphore()
    for axis, me, count in (("gx", me_x, count_x), ("gy", me_y, count_y)):
        for step in range(1, count):
            pl.semaphore_signal(
                barrier, inc=1, device_id={axis: lax.rem(me + step, count)}, device_id_type=MESH
            )
    own = [
        pltpu.make_async_copy(parts_x.at[me_x], got_x.at[me_x], recv_x.at[0]),
        pltpu.make_async_copy(parts_y.at[me_y], got_y.at[me_y], recv_y.at[0]),
    ]
    for copy in own:
        copy.start()
    pl.semaphore_wait(barrier, count_x + count_y - 2)
    groups = []
    for axis, me, count, parts, got, send, recv in (
        ("gx", me_x, count_x, parts_x, got_x, send_x, recv_x),
        ("gy", me_y, count_y, parts_y, got_y, send_y, recv_y),
    ):
        groups.append([
            exchange_copy(parts, got, send, recv, axis, me, count, step) for step in range(1, count)
        ])
        for copy in groups[-1]:
            copy.start()
    for group, family, count, got, image in (
        (groups[1], 1, count_y, got_y, image_y),
        (groups[0], 0, count_x, got_x, image_x),
    ):
        for copy in group:
            copy.wait_recv()
        own[family].wait()
        compose(got, direction, family, count, views, image)
    for group in groups:
        for copy in group:
            copy.wait_send()


def local(density, transfer_table, shear_x, shear_y, direction):
    count_x, count_y = lax.axis_size("gx"), lax.axis_size("gy")
    counts = (count_x, count_y)
    dims = density.shape
    depth_x, depth_y, cells_z = dims
    views = shear_x.shape[0]
    f32 = jnp.float32
    piece_x, piece_y = depth_y // count_x, depth_x // count_y
    cells = depth_x * depth_y
    vmem = pl.BlockSpec(memory_space=pltpu.VMEM)
    smem = pl.BlockSpec(memory_space=pltpu.SMEM)
    far = pl.BlockSpec(memory_space=pl.ANY)
    density = density.reshape(cells, cells_z)
    layer_x = jax.ShapeDtypeStruct((depth_y, cells_z), f32)
    layer_y = jax.ShapeDtypeStruct((depth_x, cells_z), f32)
    halos = pl.pallas_call(
        functools.partial(halo_kernel, dims, counts),
        out_shape=(layer_x, layer_x, layer_y, layer_y),
        in_specs=[vmem],
        out_specs=(vmem,) * 4,
        scratch_shapes=[
            pltpu.VMEM((depth_x, cells_z), f32),
            pltpu.VMEM((depth_x, cells_z), f32),
            pltpu.SemaphoreType.DMA((4,)),
            pltpu.SemaphoreType.DMA((4,)),
        ],
        compiler_params=pltpu.CompilerParams(collective_id=0, has_side_effects=True),
    )(density)
    parts = pl.pallas_call(
        functools.partial(brick_kernel, dims, counts),
        out_shape=(
            jax.ShapeDtypeStruct((count_x, views * 4, piece_x, cells_z), f32),
            jax.ShapeDtypeStruct((count_y, views * 4, piece_y, cells_z), f32),
        ),
        in_specs=[far, vmem, smem, smem, smem] + [far] * 4,
        out_specs=(vmem, vmem),
        scratch_shapes=[
            pltpu.VMEM((4, cells, cells_z), f32),
            pltpu.VMEM((4, cells, cells_z), f32),
            pltpu.VMEM((cells, cells_z), f32),
            pltpu.VMEM((depth_y, cells_z), f32),
            pltpu.VMEM((depth_y, cells_z), f32),
            pltpu.VMEM((depth_x, cells_z), f32),
            pltpu.VMEM((depth_x, cells_z), f32),
            pltpu.SemaphoreType.DMA((5,)),
        ],
        compiler_params=pltpu.CompilerParams(vmem_limit_bytes=40 * 2**20),
    )(density, transfer_table, shear_x, shear_y, direction, *halos)
    return tuple(pl.pallas_call(
        functools.partial(compose_kernel, counts, views),
        out_shape=(
            jax.ShapeDtypeStruct((views, 4, piece_x, cells_z), f32),
            jax.ShapeDtypeStruct((views, 4, piece_y, cells_z), f32),
        ),
        in_specs=[smem, far, far],
        out_specs=(vmem, vmem),
        scratch_shapes=[
            pltpu.VMEM((count_x, views * 4, piece_x, cells_z), f32),
            pltpu.VMEM((count_y, views * 4, piece_y, cells_z), f32),
            pltpu.SemaphoreType.DMA((count_x,)),
            pltpu.SemaphoreType.DMA((count_x,)),
            pltpu.SemaphoreType.DMA((count_y,)),
            pltpu.SemaphoreType.DMA((count_y,)),
        ],
        compiler_params=pltpu.CompilerParams(collective_id=1, has_side_effects=True),
    )(direction, *parts))


def solution(mesh):
    placed = (P("gx", "gy", None), P(), P(None, "gx"), P(None, "gy"), P())
    return jax.shard_map(
        local,
        mesh=mesh,
        in_specs=placed,
        out_specs=(P(None, None, ("gy", "gx"), None), P(None, None, ("gx", "gy"), None)),
        check_vma=False,
    )
```

```python
import functools
import math

import jax
import jax.numpy as jnp
from jax import lax
from jax.experimental import pallas as pl
from jax.experimental.pallas import tpu as pltpu
from jax.sharding import PartitionSpec as P

MESH = pl.DeviceIdType.MESH
LOG2E = math.log2(math.e)
UNROLL = 16


def take(row, places):
    return jnp.take_along_axis(
        jnp.broadcast_to(row, places.shape), places, axis=1, mode="promise_in_bounds"
    )


def exchange_copy(parts, received, send_sem, recv_sem, axis, me, count, step):
    target = lax.rem(me + step, count)
    return pltpu.make_async_remote_copy(
        src_ref=parts.at[target],
        dst_ref=received.at[me],
        send_sem=send_sem.at[step],
        recv_sem=recv_sem.at[step],
        device_id={axis: target},
        device_id_type=MESH,
    )


def march(fields, shear_ref, direction_ref, family, view, depth, pitch, begin, rows, cells_z):
    lanes = lax.broadcasted_iota(jnp.int32, (rows, cells_z), 1)
    upwards = jnp.full((rows, cells_z), direction_ref[family, view], jnp.int32) == 0

    def step(i, carried):
        behind, colours = carried
        shift = shear_ref[view, i]
        amount = jnp.where(shift < 0, shift + cells_z, shift)
        inside = (lanes >= shift) & (lanes < cells_z + shift)
        at = pl.ds(pl.multiple_of(i * pitch + begin, 8), rows)
        sheared = [pltpu.roll(fields[c, at, :], amount, 1) for c in range(4)]
        optical = jnp.where(inside, sheared[3], 0.0)
        through = jnp.exp2(-jnp.where(upwards, behind, optical))
        kept = jnp.where(upwards, 1.0, through)
        added = jnp.where(inside, jnp.where(upwards, through, 1.0), 0.0)
        colours = tuple(total * kept + added * sheared[c] for c, total in enumerate(colours))
        return behind + optical, colours

    zero = jnp.zeros((rows, cells_z), jnp.float32)
    return lax.fori_loop(0, depth, step, (zero, (zero, zero, zero)), unroll=UNROLL)


def compose(received, direction_ref, family, count, views, out_ref):
    for view in range(views):
        turned = direction_ref[family, view].astype(jnp.float32)
        depths = [received[i, view * 4 + 3] for i in range(count)]
        lower, upper = [jnp.zeros_like(depths[0])], [jnp.zeros_like(depths[0])]
        for i in range(count):
            lower.append(lower[-1] + depths[i])
            upper.append(upper[-1] + depths[count - 1 - i])
        through = [
            jnp.exp2(-(lower[i] * (1.0 - turned) + upper[count - 1 - i] * turned))
            for i in range(count)
        ]
        for c in range(3):
            total = through[0] * received[0, view * 4 + c]
            for i in range(1, count):
                total += through[i] * received[i, view * 4 + c]
            out_ref[view, c] = total
        out_ref[view, 3] = 1.0 - jnp.exp2(-lower[-1])


def classify_kernel(rows, step, density, table, classed):
    knots = table.shape[1]
    levels = table[...].astype(jnp.float32) * (1.0 / 255.0)
    rises = pltpu.roll(levels, knots - 1, 1) - levels

    def classify(x, _):
        at = pl.ds(pl.multiple_of(x * rows, 8), rows)
        scaled = density[at, :] * (knots - 1.0)
        places = jnp.minimum(scaled.astype(jnp.int32), knots - 1)
        rest = scaled - places.astype(jnp.float32)
        for c in range(4):
            value = take(levels[c:c + 1], places) + rest * take(rises[c:c + 1], places)
            classed[c, at, :] = value if c < 3 else value * step
        return 0

    lax.fori_loop(0, density.shape[0] // rows, classify, 0, unroll=2)


def kernel(
    dims, counts,
    density, classed, shear_x, shear_y, direction,
    image_x, image_y,
    fields_x, fields_y, face_low, face_high,
    halo_x_low, halo_x_high, halo_y_low, halo_y_high,
    parts_x, got_x, parts_y, got_y,
    halo_send, halo_recv, send_x, recv_x, send_y, recv_y, load_sem,
):
    depth_x, depth_y, cells_z = dims
    count_x, count_y = counts
    views = shear_x.shape[0]
    me_x, me_y = lax.axis_index("gx"), lax.axis_index("gy")

    loading = pltpu.make_async_copy(classed, fields_x, load_sem)
    loading.start()
    barrier = pltpu.get_barrier_semaphore()
    for axis, me, count in (("gx", me_x, count_x), ("gy", me_y, count_y)):
        for step in range(1, count):
            pl.semaphore_signal(
                barrier, inc=1, device_id={axis: lax.rem(me + step, count)}, device_id_type=MESH
            )
    face_low[...] = density[pl.ds(0, depth_x, stride=depth_y), :]
    face_high[...] = density[pl.ds(depth_y - 1, depth_x, stride=depth_y), :]
    pl.semaphore_wait(barrier, count_x + count_y - 2)

    last = (depth_x - 1) * depth_y
    halos = []
    for k, (axis, me, count, delta, src, dst) in enumerate((
        ("gx", me_x, count_x, 1, density.at[pl.ds(last, depth_y), :], halo_x_low),
        ("gx", me_x, count_x, -1, density.at[pl.ds(0, depth_y), :], halo_x_high),
        ("gy", me_y, count_y, 1, face_high, halo_y_low),
        ("gy", me_y, count_y, -1, face_low, halo_y_high),
    )):
        copy = pltpu.make_async_remote_copy(
            src_ref=src, dst_ref=dst, send_sem=halo_send.at[k], recv_sem=halo_recv.at[k],
            device_id={axis: lax.rem(me + delta + count, count)}, device_id_type=MESH,
        )
        sends = me < count - 1 if delta == 1 else me > 0
        receives = me > 0 if delta == 1 else me < count - 1
        halos.append((copy, sends, receives, dst))
        pl.when(sends)(copy.start)

    step_x = 2.0 * LOG2E / (depth_x * count_x)
    step_y = 2.0 * LOG2E / (depth_y * count_y)

    loading.wait()

    def turn(x, _):
        at = pl.ds(pl.multiple_of(x * depth_y, 8), depth_y)
        fields_y[3, pl.ds(x, depth_y, stride=depth_x), :] = fields_x[3, at, :] * (step_y / step_x)
        return 0

    lax.fori_loop(0, depth_x, turn, 0, unroll=2)

    for copy, sends, receives, dst in halos:
        pl.when(receives)(copy.wait_recv)

        @pl.when(jnp.logical_not(receives))
        def _():
            dst[...] = jnp.zeros_like(dst)

    lanes = lax.broadcasted_iota(jnp.int32, (depth_y, cells_z), 1)
    ranks = lax.broadcasted_iota(jnp.int32, (depth_y, cells_z), 0)

    def shade(x, before, here, after):
        low = halo_y_low[pl.ds(x, 1), :]
        high = halo_y_high[pl.ds(x, 1), :]
        rise_x = after - before
        rise_y = jnp.where(ranks == depth_y - 1, high, pltpu.roll(here, depth_y - 1, 0)) - jnp.where(
            ranks == 0, low, pltpu.roll(here, 1, 0)
        )
        rise_z = jnp.where(lanes == cells_z - 1, 0.0, pltpu.roll(here, cells_z - 1, 1)) - jnp.where(
            lanes == 0, 0.0, pltpu.roll(here, 1, 1)
        )
        facing = jnp.abs(rise_x + 2.0 * (rise_y + rise_z)) * (0.7 / 3.0)
        steep = rise_x * rise_x + rise_y * rise_y + rise_z * rise_z + 0.04
        shaded = 0.3 + facing * lax.rsqrt(steep)
        at = pl.ds(pl.multiple_of(x * depth_y, 8), depth_y)
        turned_at = pl.ds(x, depth_y, stride=depth_x)
        optical = fields_x[3, at, :]
        gain_x = shaded * (1.0 - jnp.exp2(-optical))
        if step_x == step_y:
            gain_y = gain_x
        else:
            gain_y = shaded * (1.0 - jnp.exp2(-(optical * (step_y / step_x))))
        for c in range(3):
            colour = fields_x[c, at, :]
            fields_x[c, at, :] = colour * gain_x
            fields_y[c, turned_at, :] = colour * gain_y

    def plane(x):
        return density[pl.ds(pl.multiple_of(x * depth_y, 8), depth_y), :]

    def shade_inner(x, _):
        shade(x, plane(x - 1), plane(x), plane(x + 1))
        return 0

    shade(0, halo_x_low[...], plane(0), plane(1))
    lax.fori_loop(1, depth_x - 1, shade_inner, 0, unroll=2)
    shade(depth_x - 1, plane(depth_x - 2), plane(depth_x - 1), halo_x_high[...])

    copies = []
    for fields, shear, family, axis, me, count, depth, across, parts, got, send, recv in (
        (fields_x, shear_x, 0, "gx", me_x, count_x, depth_x, depth_y, parts_x, got_x, send_x, recv_x),
        (fields_y, shear_y, 1, "gy", me_y, count_y, depth_y, depth_x, parts_y, got_y, send_y, recv_y),
    ):
        piece = across // count
        rows = math.gcd(across, 32)
        for view in range(views):
            for begin in range(0, across, rows):
                behind, colours = march(
                    fields, shear, direction, family, view, depth, across, begin, rows, cells_z
                )
                for c, result in enumerate(colours + (behind,)):
                    for r in range(0, rows, piece):
                        parts[(begin + r) // piece, view * 4 + c] = result[r:r + piece]
        group = [
            exchange_copy(parts, got, send, recv, axis, me, count, step) for step in range(1, count)
        ]
        for copy in group:
            copy.start()
        got[me] = parts[me]
        copies.append(group)

    for copy in copies[0]:
        copy.wait_recv()
    compose(got_x, direction, 0, count_x, views, image_x)
    for copy in copies[1]:
        copy.wait_recv()
    compose(got_y, direction, 1, count_y, views, image_y)

    for copy, sends, receives, dst in halos:
        pl.when(sends)(copy.wait_send)
    for group in copies:
        for copy in group:
            copy.wait_send()


def local(density, transfer_table, shear_x, shear_y, direction):
    count_x, count_y = lax.axis_size("gx"), lax.axis_size("gy")
    depth_x, depth_y, cells_z = density.shape
    views = shear_x.shape[0]
    f32 = jnp.float32
    piece_x, piece_y = depth_y // count_x, depth_x // count_y
    cells = depth_x * depth_y
    vmem = pl.BlockSpec(memory_space=pltpu.VMEM)
    smem = pl.BlockSpec(memory_space=pltpu.SMEM)
    density = density.reshape(cells, cells_z)
    layers = math.gcd(depth_x, 8)
    classed = pl.pallas_call(
        functools.partial(classify_kernel, depth_y, 2.0 * LOG2E / (depth_x * count_x)),
        grid=(depth_x // layers,),
        out_shape=jax.ShapeDtypeStruct((4, cells, cells_z), f32),
        in_specs=[
            pl.BlockSpec((layers * depth_y, cells_z), lambda i: (i, 0)),
            pl.BlockSpec(transfer_table.shape, lambda i: (0, 0)),
        ],
        out_specs=pl.BlockSpec((4, layers * depth_y, cells_z), lambda i: (0, i, 0)),
    )(density, transfer_table)
    return tuple(pl.pallas_call(
        functools.partial(kernel, (depth_x, depth_y, cells_z), (count_x, count_y)),
        out_shape=(
            jax.ShapeDtypeStruct((views, 4, piece_x, cells_z), f32),
            jax.ShapeDtypeStruct((views, 4, piece_y, cells_z), f32),
        ),
        in_specs=[vmem, pl.BlockSpec(memory_space=pltpu.HBM), smem, smem, smem],
        out_specs=(vmem, vmem),
        scratch_shapes=[
            pltpu.VMEM((4, cells, cells_z), f32),
            pltpu.VMEM((4, cells, cells_z), f32),
            pltpu.VMEM((depth_x, cells_z), f32),
            pltpu.VMEM((depth_x, cells_z), f32),
            pltpu.VMEM((depth_y, cells_z), f32),
            pltpu.VMEM((depth_y, cells_z), f32),
            pltpu.VMEM((depth_x, cells_z), f32),
            pltpu.VMEM((depth_x, cells_z), f32),
            pltpu.VMEM((count_x, views * 4, piece_x, cells_z), f32),
            pltpu.VMEM((count_x, views * 4, piece_x, cells_z), f32),
            pltpu.VMEM((count_y, views * 4, piece_y, cells_z), f32),
            pltpu.VMEM((count_y, views * 4, piece_y, cells_z), f32),
            pltpu.SemaphoreType.DMA((4,)),
            pltpu.SemaphoreType.DMA((4,)),
            pltpu.SemaphoreType.DMA((count_x,)),
            pltpu.SemaphoreType.DMA((count_x,)),
            pltpu.SemaphoreType.DMA((count_y,)),
            pltpu.SemaphoreType.DMA((count_y,)),
            pltpu.SemaphoreType.DMA,
        ],
        compiler_params=pltpu.CompilerParams(
            collective_id=0, has_side_effects=True, vmem_limit_bytes=40 * 2**20
        ),
    )(density, classed, shear_x, shear_y, direction))


def solution(mesh):
    placed = (P("gx", "gy", None), P(), P(None, "gx"), P(None, "gy"), P())
    return jax.shard_map(
        local,
        mesh=mesh,
        in_specs=placed,
        out_specs=(P(None, None, ("gy", "gx"), None), P(None, None, ("gx", "gy"), None)),
        check_vma=False,
    )
```

```python
import functools
import math

import jax
import jax.numpy as jnp
from jax import lax
from jax.experimental import pallas as pl
from jax.experimental.pallas import tpu as pltpu
from jax.sharding import PartitionSpec as P

MESH = pl.DeviceIdType.MESH
LOG2E = math.log2(math.e)
UNROLL = 16


def take(row, places):
    return jnp.take_along_axis(
        jnp.broadcast_to(row, places.shape), places, axis=1, mode="promise_in_bounds"
    )


def exchange_copy(parts, received, send_sem, recv_sem, axis, me, count, step):
    target = lax.rem(me + step, count)
    return pltpu.make_async_remote_copy(
        src_ref=parts.at[target],
        dst_ref=received.at[me],
        send_sem=send_sem.at[step],
        recv_sem=recv_sem.at[step],
        device_id={axis: target},
        device_id_type=MESH,
    )


def march(fields, shear_ref, direction_ref, family, view, depth, pitch, begin, rows, cells_z):
    lanes = lax.broadcasted_iota(jnp.int32, (rows, cells_z), 1)
    upwards = jnp.full((rows, cells_z), direction_ref[family, view], jnp.int32) == 0

    def step(i, carried):
        behind, colours = carried
        shift = shear_ref[view, i]
        amount = jnp.where(shift < 0, shift + cells_z, shift)
        inside = (lanes >= shift) & (lanes < cells_z + shift)
        at = pl.ds(pl.multiple_of(i * pitch + begin, 8), rows)
        sheared = [pltpu.roll(fields[c, at, :], amount, 1) for c in range(4)]
        optical = jnp.where(inside, sheared[3], 0.0)
        through = jnp.exp2(-jnp.where(upwards, behind, optical))
        kept = jnp.where(upwards, 1.0, through)
        added = jnp.where(inside, jnp.where(upwards, through, 1.0), 0.0)
        colours = tuple(total * kept + added * sheared[c] for c, total in enumerate(colours))
        return behind + optical, colours

    zero = jnp.zeros((rows, cells_z), jnp.float32)
    return lax.fori_loop(0, depth, step, (zero, (zero, zero, zero)), unroll=UNROLL)


def compose(received, direction_ref, family, count, views, out_ref):
    for view in range(views):
        turned = direction_ref[family, view].astype(jnp.float32)
        depths = [received[i, view * 4 + 3] for i in range(count)]
        lower, upper = [jnp.zeros_like(depths[0])], [jnp.zeros_like(depths[0])]
        for i in range(count):
            lower.append(lower[-1] + depths[i])
            upper.append(upper[-1] + depths[count - 1 - i])
        through = [
            jnp.exp2(-(lower[i] * (1.0 - turned) + upper[count - 1 - i] * turned))
            for i in range(count)
        ]
        for c in range(3):
            total = through[0] * received[0, view * 4 + c]
            for i in range(1, count):
                total += through[i] * received[i, view * 4 + c]
            out_ref[view, c] = total
        out_ref[view, 3] = 1.0 - jnp.exp2(-lower[-1])


def classify(density, table, scales):
    knots = table.shape[1]
    packed = table[3:4] * 2**24 + table[2:3] * 2**16 + table[1:2] * 2**8 + table[0:1]
    scaled = density * (knots - 1.0)
    places = jnp.minimum(scaled.astype(jnp.int32), knots - 1)
    rest = scaled - places.astype(jnp.float32)
    low, high = take(packed, places), take(pltpu.roll(packed, knots - 1, 1), places)
    values = []
    for c in range(4):
        lower = (lax.shift_right_logical(low, 8 * c) & 255).astype(jnp.float32)
        upper = (lax.shift_right_logical(high, 8 * c) & 255).astype(jnp.float32)
        values.append((lower + rest * (upper - lower)) * scales[c])
    return values


def kernel(
    dims, counts,
    density_far, table, shear_x, shear_y, direction,
    image_x, image_y,
    fields_x, fields_y, face_low, face_high,
    halo_x_low, halo_x_high, halo_y_low, halo_y_high,
    parts_x, got_x, parts_y, got_y,
    halo_send, halo_recv, send_x, recv_x, send_y, recv_y, density, load_sem,
):
    depth_x, depth_y, cells_z = dims
    count_x, count_y = counts
    views = shear_x.shape[0]
    me_x, me_y = lax.axis_index("gx"), lax.axis_index("gy")

    quarter = density.shape[0] // 4
    loading = [
        pltpu.make_async_copy(
            density_far.at[pl.ds(k * quarter, quarter), :],
            density.at[pl.ds(k * quarter, quarter), :], load_sem.at[k],
        )
        for k in range(4)
    ]
    for copy in loading:
        copy.start()
    barrier = pltpu.get_barrier_semaphore()
    for axis, me, count in (("gx", me_x, count_x), ("gy", me_y, count_y)):
        for step in range(1, count):
            pl.semaphore_signal(
                barrier, inc=1, device_id={axis: lax.rem(me + step, count)}, device_id_type=MESH
            )
    for copy in loading:
        copy.wait()
    face_low[...] = density[pl.ds(0, depth_x, stride=depth_y), :]
    face_high[...] = density[pl.ds(depth_y - 1, depth_x, stride=depth_y), :]
    pl.semaphore_wait(barrier, count_x + count_y - 2)

    last = (depth_x - 1) * depth_y
    halos = []
    for k, (axis, me, count, delta, src, dst) in enumerate((
        ("gx", me_x, count_x, 1, density.at[pl.ds(last, depth_y), :], halo_x_low),
        ("gx", me_x, count_x, -1, density.at[pl.ds(0, depth_y), :], halo_x_high),
        ("gy", me_y, count_y, 1, face_high, halo_y_low),
        ("gy", me_y, count_y, -1, face_low, halo_y_high),
    )):
        copy = pltpu.make_async_remote_copy(
            src_ref=src, dst_ref=dst, send_sem=halo_send.at[k], recv_sem=halo_recv.at[k],
            device_id={axis: lax.rem(me + delta + count, count)}, device_id_type=MESH,
        )
        sends = me < count - 1 if delta == 1 else me > 0
        receives = me > 0 if delta == 1 else me < count - 1
        halos.append((copy, sends, receives, dst))
        pl.when(sends)(copy.start)

    step_x = 2.0 * LOG2E / (depth_x * count_x)
    step_y = 2.0 * LOG2E / (depth_y * count_y)

    levels = table[...]
    scales = (1.0 / 255.0, 1.0 / 255.0, 1.0 / 255.0, step_x / 255.0)

    def look_up(x, _):
        at = pl.ds(pl.multiple_of(x * depth_y, 8), depth_y)
        values = classify(density[at, :], levels, scales)
        for c in range(4):
            fields_x[c, at, :] = values[c]
        fields_y[3, pl.ds(x, depth_y, stride=depth_x), :] = values[3] * (step_y / step_x)
        return 0

    lax.fori_loop(0, depth_x, look_up, 0, unroll=2)

    for copy, sends, receives, dst in halos:
        pl.when(receives)(copy.wait_recv)

        @pl.when(jnp.logical_not(receives))
        def _():
            dst[...] = jnp.zeros_like(dst)

    lanes = lax.broadcasted_iota(jnp.int32, (depth_y, cells_z), 1)
    ranks = lax.broadcasted_iota(jnp.int32, (depth_y, cells_z), 0)

    def shade(x, before, here, after):
        low = halo_y_low[pl.ds(x, 1), :]
        high = halo_y_high[pl.ds(x, 1), :]
        rise_x = after - before
        rise_y = jnp.where(ranks == depth_y - 1, high, pltpu.roll(here, depth_y - 1, 0)) - jnp.where(
            ranks == 0, low, pltpu.roll(here, 1, 0)
        )
        rise_z = jnp.where(lanes == cells_z - 1, 0.0, pltpu.roll(here, cells_z - 1, 1)) - jnp.where(
            lanes == 0, 0.0, pltpu.roll(here, 1, 1)
        )
        facing = jnp.abs(rise_x + 2.0 * (rise_y + rise_z)) * (0.7 / 3.0)
        steep = rise_x * rise_x + rise_y * rise_y + rise_z * rise_z + 0.04
        shaded = 0.3 + facing * lax.rsqrt(steep)
        at = pl.ds(pl.multiple_of(x * depth_y, 8), depth_y)
        turned_at = pl.ds(x, depth_y, stride=depth_x)
        optical = fields_x[3, at, :]
        gain_x = shaded * (1.0 - jnp.exp2(-optical))
        if step_x == step_y:
            gain_y = gain_x
        else:
            gain_y = shaded * (1.0 - jnp.exp2(-(optical * (step_y / step_x))))
        for c in range(3):
            colour = fields_x[c, at, :]
            fields_x[c, at, :] = colour * gain_x
            fields_y[c, turned_at, :] = colour * gain_y

    def plane(x):
        return density[pl.ds(pl.multiple_of(x * depth_y, 8), depth_y), :]

    def shade_inner(x, _):
        shade(x, plane(x - 1), plane(x), plane(x + 1))
        return 0

    shade(0, halo_x_low[...], plane(0), plane(1))
    lax.fori_loop(1, depth_x - 1, shade_inner, 0, unroll=2)
    shade(depth_x - 1, plane(depth_x - 2), plane(depth_x - 1), halo_x_high[...])

    copies = []
    for fields, shear, family, axis, me, count, depth, across, parts, got, send, recv in (
        (fields_x, shear_x, 0, "gx", me_x, count_x, depth_x, depth_y, parts_x, got_x, send_x, recv_x),
        (fields_y, shear_y, 1, "gy", me_y, count_y, depth_y, depth_x, parts_y, got_y, send_y, recv_y),
    ):
        piece = across // count
        rows = math.gcd(across, 32)
        for view in range(views):
            for begin in range(0, across, rows):
                behind, colours = march(
                    fields, shear, direction, family, view, depth, across, begin, rows, cells_z
                )
                for c, result in enumerate(colours + (behind,)):
                    for r in range(0, rows, piece):
                        parts[(begin + r) // piece, view * 4 + c] = result[r:r + piece]
        group = [
            exchange_copy(parts, got, send, recv, axis, me, count, step) for step in range(1, count)
        ]
        for copy in group:
            copy.start()
        got[me] = parts[me]
        copies.append(group)

    for copy in copies[0]:
        copy.wait_recv()
    compose(got_x, direction, 0, count_x, views, image_x)
    for copy in copies[1]:
        copy.wait_recv()
    compose(got_y, direction, 1, count_y, views, image_y)

    for copy, sends, receives, dst in halos:
        pl.when(sends)(copy.wait_send)
    for group in copies:
        for copy in group:
            copy.wait_send()


def local(density, transfer_table, shear_x, shear_y, direction):
    count_x, count_y = lax.axis_size("gx"), lax.axis_size("gy")
    depth_x, depth_y, cells_z = density.shape
    views = shear_x.shape[0]
    f32 = jnp.float32
    piece_x, piece_y = depth_y // count_x, depth_x // count_y
    cells = depth_x * depth_y
    vmem = pl.BlockSpec(memory_space=pltpu.VMEM)
    smem = pl.BlockSpec(memory_space=pltpu.SMEM)
    density = density.reshape(cells, cells_z)
    return tuple(pl.pallas_call(
        functools.partial(kernel, (depth_x, depth_y, cells_z), (count_x, count_y)),
        out_shape=(
            jax.ShapeDtypeStruct((views, 4, piece_x, cells_z), f32),
            jax.ShapeDtypeStruct((views, 4, piece_y, cells_z), f32),
        ),
        in_specs=[pl.BlockSpec(memory_space=pltpu.HBM), vmem, smem, smem, smem],
        out_specs=(vmem, vmem),
        scratch_shapes=[
            pltpu.VMEM((4, cells, cells_z), f32),
            pltpu.VMEM((4, cells, cells_z), f32),
            pltpu.VMEM((depth_x, cells_z), f32),
            pltpu.VMEM((depth_x, cells_z), f32),
            pltpu.VMEM((depth_y, cells_z), f32),
            pltpu.VMEM((depth_y, cells_z), f32),
            pltpu.VMEM((depth_x, cells_z), f32),
            pltpu.VMEM((depth_x, cells_z), f32),
            pltpu.VMEM((count_x, views * 4, piece_x, cells_z), f32),
            pltpu.VMEM((count_x, views * 4, piece_x, cells_z), f32),
            pltpu.VMEM((count_y, views * 4, piece_y, cells_z), f32),
            pltpu.VMEM((count_y, views * 4, piece_y, cells_z), f32),
            pltpu.SemaphoreType.DMA((4,)),
            pltpu.SemaphoreType.DMA((4,)),
            pltpu.SemaphoreType.DMA((count_x,)),
            pltpu.SemaphoreType.DMA((count_x,)),
            pltpu.SemaphoreType.DMA((count_y,)),
            pltpu.SemaphoreType.DMA((count_y,)),
            pltpu.VMEM((cells, cells_z), f32),
            pltpu.SemaphoreType.DMA((4,)),
        ],
        compiler_params=pltpu.CompilerParams(
            collective_id=0, has_side_effects=True, vmem_limit_bytes=40 * 2**20
        ),
    )(density, transfer_table, shear_x, shear_y, direction))


def solution(mesh):
    placed = (P("gx", "gy", None), P(), P(None, "gx"), P(None, "gy"), P())
    return jax.shard_map(
        local,
        mesh=mesh,
        in_specs=placed,
        out_specs=(P(None, None, ("gy", "gx"), None), P(None, None, ("gx", "gy"), None)),
        check_vma=False,
    )
```

```python
import functools
import math

import jax
import jax.numpy as jnp
from jax import lax
from jax.experimental import pallas as pl
from jax.experimental.pallas import tpu as pltpu
from jax.sharding import PartitionSpec as P

MESH = pl.DeviceIdType.MESH
LOG2E = math.log2(math.e)
UNROLL = 16


def take(row, places):
    return jnp.take_along_axis(
        jnp.broadcast_to(row, places.shape), places, axis=1, mode="promise_in_bounds"
    )


def exchange_copy(parts, received, send_sem, recv_sem, axis, me, count, step):
    target = lax.rem(me + step, count)
    return pltpu.make_async_remote_copy(
        src_ref=parts.at[target],
        dst_ref=received.at[me],
        send_sem=send_sem.at[step],
        recv_sem=recv_sem.at[step],
        device_id={axis: target},
        device_id_type=MESH,
    )


def march(fields, shear_ref, direction_ref, family, view, depth, pitch, begin, rows, cells_z):
    lanes = lax.broadcasted_iota(jnp.int32, (rows, cells_z), 1)
    upwards = jnp.full((rows, cells_z), direction_ref[family, view], jnp.int32) == 0

    def step(i, carried):
        behind, colours = carried
        shift = shear_ref[view, i]
        amount = jnp.where(shift < 0, shift + cells_z, shift)
        inside = (lanes >= shift) & (lanes < cells_z + shift)
        at = pl.ds(pl.multiple_of(i * pitch + begin, 8), rows)
        sheared = [pltpu.roll(fields[c, at, :], amount, 1) for c in range(4)]
        optical = jnp.where(inside, sheared[3], 0.0)
        through = jnp.exp2(-jnp.where(upwards, behind, optical))
        kept = jnp.where(upwards, 1.0, through)
        added = jnp.where(inside, jnp.where(upwards, through, 1.0), 0.0)
        colours = tuple(total * kept + added * sheared[c] for c, total in enumerate(colours))
        return behind + optical, colours

    zero = jnp.zeros((rows, cells_z), jnp.float32)
    return lax.fori_loop(0, depth, step, (zero, (zero, zero, zero)), unroll=UNROLL)


def compose(received, direction_ref, family, count, views, out_ref):
    for view in range(views):
        turned = direction_ref[family, view].astype(jnp.float32)
        depths = [received[i, view * 4 + 3] for i in range(count)]
        lower, upper = [jnp.zeros_like(depths[0])], [jnp.zeros_like(depths[0])]
        for i in range(count):
            lower.append(lower[-1] + depths[i])
            upper.append(upper[-1] + depths[count - 1 - i])
        through = [
            jnp.exp2(-(lower[i] * (1.0 - turned) + upper[count - 1 - i] * turned))
            for i in range(count)
        ]
        for c in range(3):
            total = through[0] * received[0, view * 4 + c]
            for i in range(1, count):
                total += through[i] * received[i, view * 4 + c]
            out_ref[view, c] = total
        out_ref[view, 3] = 1.0 - jnp.exp2(-lower[-1])


def classify(density, table, scales):
    knots = table.shape[1]
    packed = table[3:4] * 2**24 + table[2:3] * 2**16 + table[1:2] * 2**8 + table[0:1]
    scaled = density * (knots - 1.0)
    places = jnp.minimum(scaled.astype(jnp.int32), knots - 1)
    rest = scaled - places.astype(jnp.float32)
    low, high = take(packed, places), take(pltpu.roll(packed, knots - 1, 1), places)
    values = []
    for c in range(4):
        lower = (lax.shift_right_logical(low, 8 * c) & 255).astype(jnp.float32)
        upper = (lax.shift_right_logical(high, 8 * c) & 255).astype(jnp.float32)
        values.append((lower + rest * (upper - lower)) * scales[c])
    return values


def kernel(
    dims, counts,
    density_far, table_far, shear_x_far, shear_y_far, direction_far,
    image_x, image_y,
    fields_x, fields_y, face_low, face_high,
    halo_x_low, halo_x_high, halo_y_low, halo_y_high,
    parts_x, got_x, parts_y, got_y,
    halo_send, halo_recv, send_x, recv_x, send_y, recv_y, density, table, shear_x, shear_y, direction, load_sem, small_sem,
):
    depth_x, depth_y, cells_z = dims
    count_x, count_y = counts
    views = shear_x.shape[0]
    me_x, me_y = lax.axis_index("gx"), lax.axis_index("gy")

    quarter = density.shape[0] // 4
    loading = [
        pltpu.make_async_copy(
            density_far.at[pl.ds(k * quarter, quarter), :],
            density.at[pl.ds(k * quarter, quarter), :], load_sem.at[k],
        )
        for k in range(4)
    ]
    small = [
        pltpu.make_async_copy(source, target, small_sem.at[k])
        for k, (source, target) in enumerate((
            (table_far, table), (shear_x_far, shear_x),
            (shear_y_far, shear_y), (direction_far, direction),
        ))
    ]
    for copy in loading + small:
        copy.start()
    barrier = pltpu.get_barrier_semaphore()
    for axis, me, count in (("gx", me_x, count_x), ("gy", me_y, count_y)):
        for step in range(1, count):
            pl.semaphore_signal(
                barrier, inc=1, device_id={axis: lax.rem(me + step, count)}, device_id_type=MESH
            )
    for copy in loading + small:
        copy.wait()
    face_low[...] = density[pl.ds(0, depth_x, stride=depth_y), :]
    face_high[...] = density[pl.ds(depth_y - 1, depth_x, stride=depth_y), :]
    pl.semaphore_wait(barrier, count_x + count_y - 2)

    last = (depth_x - 1) * depth_y
    halos = []
    for k, (axis, me, count, delta, src, dst) in enumerate((
        ("gx", me_x, count_x, 1, density.at[pl.ds(last, depth_y), :], halo_x_low),
        ("gx", me_x, count_x, -1, density.at[pl.ds(0, depth_y), :], halo_x_high),
        ("gy", me_y, count_y, 1, face_high, halo_y_low),
        ("gy", me_y, count_y, -1, face_low, halo_y_high),
    )):
        copy = pltpu.make_async_remote_copy(
            src_ref=src, dst_ref=dst, send_sem=halo_send.at[k], recv_sem=halo_recv.at[k],
            device_id={axis: lax.rem(me + delta + count, count)}, device_id_type=MESH,
        )
        sends = me < count - 1 if delta == 1 else me > 0
        receives = me > 0 if delta == 1 else me < count - 1
        halos.append((copy, sends, receives, dst))
        pl.when(sends)(copy.start)

    step_x = 2.0 * LOG2E / (depth_x * count_x)
    step_y = 2.0 * LOG2E / (depth_y * count_y)

    levels = table[...]
    scales = (1.0 / 255.0, 1.0 / 255.0, 1.0 / 255.0, step_x / 255.0)

    def look_up(x, _):
        at = pl.ds(pl.multiple_of(x * depth_y, 8), depth_y)
        values = classify(density[at, :], levels, scales)
        for c in range(4):
            fields_x[c, at, :] = values[c]
        fields_y[3, pl.ds(x, depth_y, stride=depth_x), :] = values[3] * (step_y / step_x)
        return 0

    lax.fori_loop(0, depth_x, look_up, 0, unroll=2)

    for copy, sends, receives, dst in halos:
        pl.when(receives)(copy.wait_recv)

        @pl.when(jnp.logical_not(receives))
        def _():
            dst[...] = jnp.zeros_like(dst)

    lanes = lax.broadcasted_iota(jnp.int32, (depth_y, cells_z), 1)
    ranks = lax.broadcasted_iota(jnp.int32, (depth_y, cells_z), 0)

    def shade(x, before, here, after):
        low = halo_y_low[pl.ds(x, 1), :]
        high = halo_y_high[pl.ds(x, 1), :]
        rise_x = after - before
        rise_y = jnp.where(ranks == depth_y - 1, high, pltpu.roll(here, depth_y - 1, 0)) - jnp.where(
            ranks == 0, low, pltpu.roll(here, 1, 0)
        )
        rise_z = jnp.where(lanes == cells_z - 1, 0.0, pltpu.roll(here, cells_z - 1, 1)) - jnp.where(
            lanes == 0, 0.0, pltpu.roll(here, 1, 1)
        )
        facing = jnp.abs(rise_x + 2.0 * (rise_y + rise_z)) * (0.7 / 3.0)
        steep = rise_x * rise_x + rise_y * rise_y + rise_z * rise_z + 0.04
        shaded = 0.3 + facing * lax.rsqrt(steep)
        at = pl.ds(pl.multiple_of(x * depth_y, 8), depth_y)
        turned_at = pl.ds(x, depth_y, stride=depth_x)
        optical = fields_x[3, at, :]
        gain_x = shaded * (1.0 - jnp.exp2(-optical))
        if step_x == step_y:
            gain_y = gain_x
        else:
            gain_y = shaded * (1.0 - jnp.exp2(-(optical * (step_y / step_x))))
        for c in range(3):
            colour = fields_x[c, at, :]
            fields_x[c, at, :] = colour * gain_x
            fields_y[c, turned_at, :] = colour * gain_y

    def plane(x):
        return density[pl.ds(pl.multiple_of(x * depth_y, 8), depth_y), :]

    def shade_inner(x, _):
        shade(x, plane(x - 1), plane(x), plane(x + 1))
        return 0

    shade(0, halo_x_low[...], plane(0), plane(1))
    lax.fori_loop(1, depth_x - 1, shade_inner, 0, unroll=2)
    shade(depth_x - 1, plane(depth_x - 2), plane(depth_x - 1), halo_x_high[...])

    copies = []
    for fields, shear, family, axis, me, count, depth, across, parts, got, send, recv in (
        (fields_x, shear_x, 0, "gx", me_x, count_x, depth_x, depth_y, parts_x, got_x, send_x, recv_x),
        (fields_y, shear_y, 1, "gy", me_y, count_y, depth_y, depth_x, parts_y, got_y, send_y, recv_y),
    ):
        piece = across // count
        rows = math.gcd(across, 32)
        for view in range(views):
            for begin in range(0, across, rows):
                behind, colours = march(
                    fields, shear, direction, family, view, depth, across, begin, rows, cells_z
                )
                for c, result in enumerate(colours + (behind,)):
                    for r in range(0, rows, piece):
                        parts[(begin + r) // piece, view * 4 + c] = result[r:r + piece]
        group = [
            exchange_copy(parts, got, send, recv, axis, me, count, step) for step in range(1, count)
        ]
        for copy in group:
            copy.start()
        got[me] = parts[me]
        copies.append(group)

    for copy in copies[0]:
        copy.wait_recv()
    compose(got_x, direction, 0, count_x, views, image_x)
    for copy in copies[1]:
        copy.wait_recv()
    compose(got_y, direction, 1, count_y, views, image_y)

    for copy, sends, receives, dst in halos:
        pl.when(sends)(copy.wait_send)
    for group in copies:
        for copy in group:
            copy.wait_send()


def local(density, transfer_table, shear_x, shear_y, direction):
    count_x, count_y = lax.axis_size("gx"), lax.axis_size("gy")
    depth_x, depth_y, cells_z = density.shape
    views = shear_x.shape[0]
    f32 = jnp.float32
    piece_x, piece_y = depth_y // count_x, depth_x // count_y
    cells = depth_x * depth_y
    vmem = pl.BlockSpec(memory_space=pltpu.VMEM)
    density = density.reshape(cells, cells_z)
    return tuple(pl.pallas_call(
        functools.partial(kernel, (depth_x, depth_y, cells_z), (count_x, count_y)),
        out_shape=(
            jax.ShapeDtypeStruct((views, 4, piece_x, cells_z), f32),
            jax.ShapeDtypeStruct((views, 4, piece_y, cells_z), f32),
        ),
        in_specs=[pl.BlockSpec(memory_space=pltpu.HBM)] * 5,
        out_specs=(vmem, vmem),
        scratch_shapes=[
            pltpu.VMEM((4, cells, cells_z), f32),
            pltpu.VMEM((4, cells, cells_z), f32),
            pltpu.VMEM((depth_x, cells_z), f32),
            pltpu.VMEM((depth_x, cells_z), f32),
            pltpu.VMEM((depth_y, cells_z), f32),
            pltpu.VMEM((depth_y, cells_z), f32),
            pltpu.VMEM((depth_x, cells_z), f32),
            pltpu.VMEM((depth_x, cells_z), f32),
            pltpu.VMEM((count_x, views * 4, piece_x, cells_z), f32),
            pltpu.VMEM((count_x, views * 4, piece_x, cells_z), f32),
            pltpu.VMEM((count_y, views * 4, piece_y, cells_z), f32),
            pltpu.VMEM((count_y, views * 4, piece_y, cells_z), f32),
            pltpu.SemaphoreType.DMA((4,)),
            pltpu.SemaphoreType.DMA((4,)),
            pltpu.SemaphoreType.DMA((count_x,)),
            pltpu.SemaphoreType.DMA((count_x,)),
            pltpu.SemaphoreType.DMA((count_y,)),
            pltpu.SemaphoreType.DMA((count_y,)),
            pltpu.VMEM((cells, cells_z), f32),
            pltpu.VMEM(transfer_table.shape, jnp.int32),
            pltpu.SMEM(shear_x.shape, jnp.int32),
            pltpu.SMEM(shear_y.shape, jnp.int32),
            pltpu.SMEM(direction.shape, jnp.int32),
            pltpu.SemaphoreType.DMA((4,)),
            pltpu.SemaphoreType.DMA((4,)),
        ],
        compiler_params=pltpu.CompilerParams(
            collective_id=0, has_side_effects=True, vmem_limit_bytes=64 * 2**20
        ),
    )(density, transfer_table, shear_x, shear_y, direction))


def solution(mesh):
    placed = (P("gx", "gy", None), P(), P(None, "gx"), P(None, "gy"), P())
    return jax.shard_map(
        local,
        mesh=mesh,
        in_specs=placed,
        out_specs=(P(None, None, ("gy", "gx"), None), P(None, None, ("gx", "gy"), None)),
        check_vma=False,
    )
```

```python
import functools
import math

import jax
import jax.numpy as jnp
from jax import lax
from jax.experimental import pallas as pl
from jax.experimental.pallas import tpu as pltpu
from jax.sharding import PartitionSpec as P

MESH = pl.DeviceIdType.MESH
LOG2E = math.log2(math.e)
UNROLL = 16


def take(row, places):
    return jnp.take_along_axis(
        jnp.broadcast_to(row, places.shape), places, axis=1, mode="promise_in_bounds"
    )


def exchange_copy(parts, received, send_sem, recv_sem, axis, me, count, step, view):
    target = lax.rem(me + step, count)
    return pltpu.make_async_remote_copy(
        src_ref=parts.at[target, pl.ds(view * 4, 4)],
        dst_ref=received.at[me, pl.ds(view * 4, 4)],
        send_sem=send_sem.at[view, step],
        recv_sem=recv_sem.at[view, step],
        device_id={axis: target},
        device_id_type=MESH,
    )


def march(fields, shear_ref, direction_ref, family, view, depth, pitch, begin, rows, cells_z):
    lanes = lax.broadcasted_iota(jnp.int32, (rows, cells_z), 1)
    turned = jnp.full((rows, cells_z), direction_ref[family, view], jnp.int32)
    upwards = turned == 0
    sign = (2 * turned - 1).astype(jnp.float32)

    def step(i, carried):
        behind, colours = carried
        shift = shear_ref[view, i]
        amount = jnp.where(shift < 0, shift + cells_z, shift)
        inside = (lanes >= shift) & (lanes < cells_z + shift)
        at = pl.ds(pl.multiple_of(i * pitch + begin, 8), rows)
        sheared = [pltpu.roll(fields[c, at, :], amount, 1) for c in range(4)]
        after = behind + jnp.where(inside, sheared[3] * sign, 0.0)
        through = jnp.where(inside, jnp.exp2(jnp.where(upwards, behind, after)), 0.0)
        colours = tuple(total + through * sheared[c] for c, total in enumerate(colours))
        return after, colours

    zero = jnp.zeros((rows, cells_z), jnp.float32)
    signed, colours = lax.fori_loop(0, depth, step, (zero, (zero, zero, zero)), unroll=UNROLL)
    summed = signed * sign
    rest = jnp.where(upwards, 1.0, jnp.exp2(-summed))
    return summed, tuple(total * rest for total in colours)


def compose(received, direction_ref, family, count, views, out_ref):
    for view in range(views):
        turned = direction_ref[family, view].astype(jnp.float32)
        depths = [received[i, view * 4 + 3] for i in range(count)]
        lower, upper = [jnp.zeros_like(depths[0])], [jnp.zeros_like(depths[0])]
        for i in range(count):
            lower.append(lower[-1] + depths[i])
            upper.append(upper[-1] + depths[count - 1 - i])
        through = [
            jnp.exp2(-(lower[i] * (1.0 - turned) + upper[count - 1 - i] * turned))
            for i in range(count)
        ]
        for c in range(3):
            total = through[0] * received[0, view * 4 + c]
            for i in range(1, count):
                total += through[i] * received[i, view * 4 + c]
            out_ref[view, c] = total
        out_ref[view, 3] = 1.0 - jnp.exp2(-lower[-1])


def classify(density, table, scales):
    knots = table.shape[1]
    packed = table[3:4] * 2**24 + table[2:3] * 2**16 + table[1:2] * 2**8 + table[0:1]
    scaled = density * (knots - 1.0)
    places = jnp.minimum(scaled.astype(jnp.int32), knots - 1)
    rest = scaled - places.astype(jnp.float32)
    low, high = take(packed, places), take(pltpu.roll(packed, knots - 1, 1), places)
    values = []
    for c in range(4):
        lower = (lax.shift_right_logical(low, 8 * c) & 255).astype(jnp.float32)
        upper = (lax.shift_right_logical(high, 8 * c) & 255).astype(jnp.float32)
        values.append((lower + rest * (upper - lower)) * scales[c])
    return values


def kernel(
    dims, counts,
    density_far, table_far, shear_x_far, shear_y_far, direction_far,
    image_x, image_y,
    fields_x, fields_y, face_low, face_high,
    halo_x_low, halo_x_high, halo_y_low, halo_y_high,
    parts_x, got_x, parts_y, got_y,
    halo_send, halo_recv, send_x, recv_x, send_y, recv_y, density, table, shear_x, shear_y, direction, load_sem, small_sem,
):
    depth_x, depth_y, cells_z = dims
    count_x, count_y = counts
    views = shear_x.shape[0]
    me_x, me_y = lax.axis_index("gx"), lax.axis_index("gy")

    quarter = density.shape[0] // 4
    loading = [
        pltpu.make_async_copy(
            density_far.at[pl.ds(k * quarter, quarter), :],
            density.at[pl.ds(k * quarter, quarter), :], load_sem.at[k],
        )
        for k in range(4)
    ]
    small = [
        pltpu.make_async_copy(source, target, small_sem.at[k])
        for k, (source, target) in enumerate((
            (table_far, table), (shear_x_far, shear_x),
            (shear_y_far, shear_y), (direction_far, direction),
        ))
    ]
    for copy in loading + small:
        copy.start()
    barrier = pltpu.get_barrier_semaphore()
    for axis, me, count in (("gx", me_x, count_x), ("gy", me_y, count_y)):
        for step in range(1, count):
            pl.semaphore_signal(
                barrier, inc=1, device_id={axis: lax.rem(me + step, count)}, device_id_type=MESH
            )
    for copy in loading + small:
        copy.wait()
    face_low[...] = density[pl.ds(0, depth_x, stride=depth_y), :]
    face_high[...] = density[pl.ds(depth_y - 1, depth_x, stride=depth_y), :]
    pl.semaphore_wait(barrier, count_x + count_y - 2)

    last = (depth_x - 1) * depth_y
    halos = []
    for k, (axis, me, count, delta, src, dst) in enumerate((
        ("gx", me_x, count_x, 1, density.at[pl.ds(last, depth_y), :], halo_x_low),
        ("gx", me_x, count_x, -1, density.at[pl.ds(0, depth_y), :], halo_x_high),
        ("gy", me_y, count_y, 1, face_high, halo_y_low),
        ("gy", me_y, count_y, -1, face_low, halo_y_high),
    )):
        copy = pltpu.make_async_remote_copy(
            src_ref=src, dst_ref=dst, send_sem=halo_send.at[k], recv_sem=halo_recv.at[k],
            device_id={axis: lax.rem(me + delta + count, count)}, device_id_type=MESH,
        )
        sends = me < count - 1 if delta == 1 else me > 0
        receives = me > 0 if delta == 1 else me < count - 1
        halos.append((copy, sends, receives, dst))
        pl.when(sends)(copy.start)

    step_x = 2.0 * LOG2E / (depth_x * count_x)
    step_y = 2.0 * LOG2E / (depth_y * count_y)

    levels = table[...]
    scales = (1.0 / 255.0, 1.0 / 255.0, 1.0 / 255.0, step_x / 255.0)

    def look_up(x, _):
        at = pl.ds(pl.multiple_of(x * depth_y, 8), depth_y)
        values = classify(density[at, :], levels, scales)
        for c in range(4):
            fields_x[c, at, :] = values[c]
        fields_y[3, pl.ds(x, depth_y, stride=depth_x), :] = values[3] * (step_y / step_x)
        return 0

    lax.fori_loop(0, depth_x, look_up, 0, unroll=2)

    for copy, sends, receives, dst in halos:
        pl.when(receives)(copy.wait_recv)

        @pl.when(jnp.logical_not(receives))
        def _():
            dst[...] = jnp.zeros_like(dst)

    lanes = lax.broadcasted_iota(jnp.int32, (depth_y, cells_z), 1)
    ranks = lax.broadcasted_iota(jnp.int32, (depth_y, cells_z), 0)

    def shade(x, before, here, after):
        low = halo_y_low[pl.ds(x, 1), :]
        high = halo_y_high[pl.ds(x, 1), :]
        rise_x = after - before
        rise_y = jnp.where(ranks == depth_y - 1, high, pltpu.roll(here, depth_y - 1, 0)) - jnp.where(
            ranks == 0, low, pltpu.roll(here, 1, 0)
        )
        rise_z = jnp.where(lanes == cells_z - 1, 0.0, pltpu.roll(here, cells_z - 1, 1)) - jnp.where(
            lanes == 0, 0.0, pltpu.roll(here, 1, 1)
        )
        facing = jnp.abs(rise_x + 2.0 * (rise_y + rise_z)) * (0.7 / 3.0)
        steep = rise_x * rise_x + rise_y * rise_y + rise_z * rise_z + 0.04
        shaded = 0.3 + facing * lax.rsqrt(steep)
        at = pl.ds(pl.multiple_of(x * depth_y, 8), depth_y)
        turned_at = pl.ds(x, depth_y, stride=depth_x)
        optical = fields_x[3, at, :]
        gain_x = shaded * (1.0 - jnp.exp2(-optical))
        if step_x == step_y:
            gain_y = gain_x
        else:
            gain_y = shaded * (1.0 - jnp.exp2(-(optical * (step_y / step_x))))
        for c in range(3):
            colour = fields_x[c, at, :]
            fields_x[c, at, :] = colour * gain_x
            fields_y[c, turned_at, :] = colour * gain_y

    def plane(x):
        return density[pl.ds(pl.multiple_of(x * depth_y, 8), depth_y), :]

    def shade_inner(x, _):
        shade(x, plane(x - 1), plane(x), plane(x + 1))
        return 0

    shade(0, halo_x_low[...], plane(0), plane(1))
    lax.fori_loop(1, depth_x - 1, shade_inner, 0, unroll=2)
    shade(depth_x - 1, plane(depth_x - 2), plane(depth_x - 1), halo_x_high[...])

    copies = []
    for fields, shear, family, axis, me, count, depth, across, parts, got, send, recv in (
        (fields_x, shear_x, 0, "gx", me_x, count_x, depth_x, depth_y, parts_x, got_x, send_x, recv_x),
        (fields_y, shear_y, 1, "gy", me_y, count_y, depth_y, depth_x, parts_y, got_y, send_y, recv_y),
    ):
        piece = across // count
        rows = math.gcd(across, 32)
        group = []
        for view in range(views):
            for begin in range(0, across, rows):
                behind, colours = march(
                    fields, shear, direction, family, view, depth, across, begin, rows, cells_z
                )
                for c, result in enumerate(colours + (behind,)):
                    for r in range(0, rows, piece):
                        parts[(begin + r) // piece, view * 4 + c] = result[r:r + piece]
            sent = [
                exchange_copy(parts, got, send, recv, axis, me, count, step, view)
                for step in range(1, count)
            ]
            for copy in sent:
                copy.start()
            group += sent
        got[me] = parts[me]
        copies.append(group)

    for copy in copies[0]:
        copy.wait_recv()
    compose(got_x, direction, 0, count_x, views, image_x)
    for copy in copies[1]:
        copy.wait_recv()
    compose(got_y, direction, 1, count_y, views, image_y)

    for copy, sends, receives, dst in halos:
        pl.when(sends)(copy.wait_send)
    for group in copies:
        for copy in group:
            copy.wait_send()


def local(density, transfer_table, shear_x, shear_y, direction):
    count_x, count_y = lax.axis_size("gx"), lax.axis_size("gy")
    depth_x, depth_y, cells_z = density.shape
    views = shear_x.shape[0]
    f32 = jnp.float32
    piece_x, piece_y = depth_y // count_x, depth_x // count_y
    cells = depth_x * depth_y
    vmem = pl.BlockSpec(memory_space=pltpu.VMEM)
    density = density.reshape(cells, cells_z)
    return tuple(pl.pallas_call(
        functools.partial(kernel, (depth_x, depth_y, cells_z), (count_x, count_y)),
        out_shape=(
            jax.ShapeDtypeStruct((views, 4, piece_x, cells_z), f32),
            jax.ShapeDtypeStruct((views, 4, piece_y, cells_z), f32),
        ),
        in_specs=[pl.BlockSpec(memory_space=pltpu.HBM)] * 5,
        out_specs=(vmem, vmem),
        scratch_shapes=[
            pltpu.VMEM((4, cells, cells_z), f32),
            pltpu.VMEM((4, cells, cells_z), f32),
            pltpu.VMEM((depth_x, cells_z), f32),
            pltpu.VMEM((depth_x, cells_z), f32),
            pltpu.VMEM((depth_y, cells_z), f32),
            pltpu.VMEM((depth_y, cells_z), f32),
            pltpu.VMEM((depth_x, cells_z), f32),
            pltpu.VMEM((depth_x, cells_z), f32),
            pltpu.VMEM((count_x, views * 4, piece_x, cells_z), f32),
            pltpu.VMEM((count_x, views * 4, piece_x, cells_z), f32),
            pltpu.VMEM((count_y, views * 4, piece_y, cells_z), f32),
            pltpu.VMEM((count_y, views * 4, piece_y, cells_z), f32),
            pltpu.SemaphoreType.DMA((4,)),
            pltpu.SemaphoreType.DMA((4,)),
            pltpu.SemaphoreType.DMA((views, count_x)),
            pltpu.SemaphoreType.DMA((views, count_x)),
            pltpu.SemaphoreType.DMA((views, count_y)),
            pltpu.SemaphoreType.DMA((views, count_y)),
            pltpu.VMEM((cells, cells_z), f32),
            pltpu.VMEM(transfer_table.shape, jnp.int32),
            pltpu.SMEM(shear_x.shape, jnp.int32),
            pltpu.SMEM(shear_y.shape, jnp.int32),
            pltpu.SMEM(direction.shape, jnp.int32),
            pltpu.SemaphoreType.DMA((4,)),
            pltpu.SemaphoreType.DMA((4,)),
        ],
        compiler_params=pltpu.CompilerParams(
            collective_id=0, has_side_effects=True, vmem_limit_bytes=64 * 2**20
        ),
    )(density, transfer_table, shear_x, shear_y, direction))


def solution(mesh):
    placed = (P("gx", "gy", None), P(), P(None, "gx"), P(None, "gy"), P())
    return jax.shard_map(
        local,
        mesh=mesh,
        in_specs=placed,
        out_specs=(P(None, None, ("gy", "gx"), None), P(None, None, ("gx", "gy"), None)),
        check_vma=False,
    )
```
